128 devices in a mesh: row: 8 (over z_hi, x), col: 16 (over z_lo, y, core).
Axes of the slice: x: 4, y: 4, z: 4 (z_hi: 2, z_lo: 2; z = z_hi * 2 + z_lo), core: 2. Of those that a mesh axis runs over, the one named last changes fastest.
Arguments:
- grad_codes: bfloat16 [16384, 3584], P(('row', 'col')), may hold values from -448 to 448
- grad_scales: bfloat16 [16384, 28], P(('row', 'col')), may hold values from 0.0039978027 to 0.039794922
- expert_ids: int32 [16384, 8], P(('row', 'col')), may hold values from 0 to 63, as said below
- slots: int32 [16384, 8], P(('row', 'col')), may hold values from 0 to 15, as said below
- gate_probs: float32 [16384, 8], P(('row', 'col')), may hold values from 0.05 to 0.5
- gate_act: bfloat16 [128, 2048, 512], P(('row', 'col')), may hold values from -6 to 6
- up_act: bfloat16 [128, 2048, 512], P(('row', 'col')), may hold values from -6 to 6
- gate_weight: bfloat16 [128, 3584, 512], P(('row', 'col')), may hold values from -0.09375 to 0.09375
- up_weight: bfloat16 [128, 3584, 512], P(('row', 'col')), may hold values from -0.09375 to 0.09375
- down_weight: bfloat16 [128, 512, 3584], P(('row', 'col')), may hold values from -0.1875 to 0.1875
Outputs:
- token_grad: bfloat16 [16384, 3584], P(('row', 'col'))
The draws below stay inside these ranges and needn't reach their ends.
Inputs may be any that keep to these rules, and one draw needn't show every extreme that they name: `expert_ids`: each token names 8 different experts, and the 128 tokens of one device name every expert exactly 16 times. On each device the experts fall into 8 sets of equal size, and column k of a token names an expert of set k. slots[t, k] is the number of earlier copies of the same device, in order of token and then of choice, that name the same expert; the copies of one device to one expert hold the slots 0 to 15, each once.
All inputs are finite; a program needn't handle non-finite values.
Results may differ from the reference program's by a relative error of at most 0.0064.
Values may be sent and summed in bfloat16 or wider, within the bound.
No kernel may reach another device: no remote copies, remote signals or barrier semaphores. Data moves between devices by JAX's collectives and lax.ppermute only.
A program may use at most 192 MiB of HBM per device.

```python
import math
import jax
import jax.numpy as jnp
from jax import lax

D = 3584
FF = 1024
QBLOCK = 128
TOPK = 8
GROUP = 2
TOK_DEV = 128
EXPERTS = 64
TOKENS = 16384
ROWS = 2048
PER = 16


def routing(key):
    groups = EXPERTS // TOPK

    def shuffle(inner_key):
        return jax.random.permutation(inner_key, TOK_DEV)

    def one_device(device_key):
        label_key, order_key = jax.random.split(device_key)
        labels = jax.random.permutation(label_key, EXPERTS).astype(jnp.int32)
        order_keys = jax.random.split(order_key, TOPK)
        orders = jax.vmap(shuffle)(order_keys).astype(jnp.int32)
        raw = jnp.arange(TOPK, dtype=jnp.int32)[:, None] * groups + orders % groups
        chosen = labels[raw].T
        flat = chosen.reshape(TOK_DEV * TOPK)
        onehot = (flat[:, None] == jnp.arange(EXPERTS, dtype=jnp.int32)[None, :]).astype(jnp.int32)
        before = jnp.cumsum(onehot, axis=0) - onehot
        rank = jnp.sum(before * onehot, axis=1)
        return (chosen, rank.reshape(TOK_DEV, TOPK))
    device_keys = jax.random.split(key, TOKENS // TOK_DEV)
    chosen, rank = lax.map(one_device, device_keys)
    return (chosen.reshape(TOKENS, TOPK).astype(jnp.int32), rank.reshape(TOKENS, TOPK).astype(jnp.int32))


def draw_expert_ids(key, part):
    shared = routing(key)
    return shared[0]


def draw_slots(key, part):
    shared = routing(key)
    return shared[1]


def steps_of(own_key, dims, pieces, low, high):
    level = 1.0
    for position, shards_of in pieces:
        heights = jax.random.uniform(jax.random.fold_in(jax.random.fold_in(own_key, 6), position), (shards_of,), jnp.float32, low / len(pieces), high / len(pieces))
        level = level * jnp.repeat(jnp.exp(heights), dims[position] // shards_of).reshape((-1,) + (1,) * (len(dims) - 1 - position))
    return level


def scatter_about(stream_key, extent, spread, reach, pieces=(), kind=jnp.bfloat16):
    level = steps_of(stream_key, extent, pieces, -0.22, 0.18) if pieces else 1.0
    drawn = jax.random.normal(stream_key, extent, jnp.float32) * spread * level
    return jnp.minimum(jnp.maximum(drawn, -reach), reach).astype(kind)


def setup_inputs(seed: int = 0) -> dict:
    streams_of = jax.random.split(jax.random.key(seed), 11)
    grad_codes = scatter_about(streams_of[0], (TOKENS, D), 64.0, 448.0, ((0, 128),))
    grad_scales = jnp.clip(jnp.exp(math.log(0.039794922) - 2.2979944 * jax.random.uniform(streams_of[1], (TOKENS, D // QBLOCK), jnp.float32) ** steps_of(streams_of[1], (TOKENS, D // QBLOCK), ((0, 128),), -0.2, 0.2)), 0.0039978027, 0.039794922).astype(jnp.bfloat16)
    expert_ids = draw_expert_ids(jax.random.fold_in(streams_of[10], 71), 0)
    slots = draw_slots(jax.random.fold_in(streams_of[10], 71), 0)
    gate_probs = jnp.clip(jnp.exp(math.log(0.5) - 2.3025851 * jax.random.uniform(streams_of[4], (TOKENS, TOPK), jnp.float32) ** steps_of(streams_of[4], (TOKENS, TOPK), ((0, 128),), -0.2, 0.2)), 0.05, 0.5)
    gate_act = scatter_about(streams_of[5], (EXPERTS * GROUP, ROWS, FF // GROUP), 1.0, 6.0, ((0, 128),))
    up_act = scatter_about(streams_of[6], (EXPERTS * GROUP, ROWS, FF // GROUP), 1.0, 6.0, ((0, 128),))
    gate_weight = scatter_about(streams_of[7], (EXPERTS * GROUP, D, FF // GROUP), D ** -0.5, 0.09375, ((0, 128),))
    up_weight = scatter_about(streams_of[8], (EXPERTS * GROUP, D, FF // GROUP), D ** -0.5, 0.09375, ((0, 128),))
    down_weight = scatter_about(streams_of[9], (EXPERTS * GROUP, FF // GROUP, D), FF ** -0.5, 0.1875, ((0, 128),))
    return {"grad_codes": grad_codes, "grad_scales": grad_scales, "expert_ids": expert_ids, "slots": slots, "gate_probs": gate_probs, "gate_act": gate_act, "up_act": up_act, "gate_weight": gate_weight, "up_weight": up_weight, "down_weight": down_weight}


def reference(grad_codes, grad_scales, expert_ids, slots, gate_probs, gate_act, up_act, gate_weight, up_weight, down_weight):
    grad = (grad_codes.astype(jnp.float32).reshape(TOKENS, D // QBLOCK, QBLOCK)
            * grad_scales.astype(jnp.float32)[:, :, None]).reshape(TOKENS, D).astype(jnp.bfloat16)
    copies = TOKENS * TOPK
    holder = jnp.arange(copies, dtype=jnp.int32) // TOPK
    device_of = holder // TOK_DEV
    places = expert_ids.reshape(copies) * ROWS + device_of * PER + slots.reshape(copies)
    source = jnp.zeros((EXPERTS * ROWS,), jnp.int32).at[places].set(holder)
    weights = jnp.zeros((EXPERTS * ROWS,), jnp.float32).at[places].set(gate_probs.reshape(copies))

    def expert_step(total, index):
        expert = index // GROUP
        start = expert * ROWS
        tokens_here = lax.dynamic_slice_in_dim(source, start, ROWS, 0)
        probs_here = lax.dynamic_slice_in_dim(weights, start, ROWS, 0)
        gate_pre = gate_act[index].astype(jnp.float32)
        up_pre = up_act[index].astype(jnp.float32)
        w_gate = gate_weight[index]
        w_up = up_weight[index]
        w_down = down_weight[index]
        sigmoid_gate = jax.nn.sigmoid(gate_pre)
        rows_grad = jnp.take(grad, tokens_here, axis=0)
        hidden_grad = jnp.dot(rows_grad, w_down.T, preferred_element_type=jnp.float32)
        gate_grad = (hidden_grad * up_pre * sigmoid_gate * (1.0 + gate_pre * (1.0 - sigmoid_gate))).astype(jnp.bfloat16)
        up_grad = (hidden_grad * gate_pre * sigmoid_gate).astype(jnp.bfloat16)
        part_grad = (jnp.dot(gate_grad, w_gate.T, preferred_element_type=jnp.float32)
                     + jnp.dot(up_grad, w_up.T, preferred_element_type=jnp.float32)).astype(jnp.bfloat16)
        total = total.at[tokens_here].add(probs_here[:, None] * part_grad.astype(jnp.float32))
        return total, None

    total, _ = lax.scan(expert_step, jnp.zeros((TOKENS, D), jnp.float32),
                        jnp.arange(EXPERTS * GROUP, dtype=jnp.int32))
    return total.astype(jnp.bfloat16)
```

```python
import functools

import jax
import jax.numpy as jnp
from jax import lax
from jax.experimental import pallas as pl
from jax.experimental.pallas import tpu as pltpu
from jax.sharding import Mesh
from jax.sharding import PartitionSpec as P

GROUP = 2
CHUNKS = 2
ROW_TILE = 256
VMEM = 56 * 1024 * 1024
SWAP = [(0, 1), (1, 0)]


def dot_nt(left, right):
    return lax.dot_general(
        left, right, (((1,), (1,)), ((), ())), preferred_element_type=jnp.float32
    )


def dot_nn(left, right):
    return jnp.dot(left, right, preferred_element_type=jnp.float32)


def dot_tn(left, right):
    return lax.dot_general(
        left, right, (((0,), (0,)), ((), ())), preferred_element_type=jnp.float32
    )


def place_of(ids_ref, slots_ref, per_chunk, rows):
    slot = slots_ref[...]
    chunk = slot // per_chunk
    return chunk * rows + ids_ref[...] * per_chunk + (slot - chunk * per_chunk)


def pick_kernel(per_chunk, rows, codes_ref, scales_ref, ids_ref, slots_ref, out_ref, grad_ref):
    tile = out_ref.shape[0]
    tokens, features = codes_ref.shape
    blocks = scales_ref.shape[1]
    width = features // blocks
    step = pl.program_id(0)

    @pl.when(step == 0)
    def _():
        for block in range(blocks):
            lanes = slice(block * width, (block + 1) * width)
            grad_ref[:, lanes] = (
                codes_ref[:, lanes].astype(jnp.float32)
                * scales_ref[:, block : block + 1].astype(jnp.float32)
            ).astype(jnp.bfloat16)

    places = place_of(ids_ref, slots_ref, per_chunk, rows)
    row = lax.broadcasted_iota(jnp.int32, (tile, tokens), 0) + step * tile
    hit = jnp.zeros((tile, tokens), jnp.float32)
    for k in range(places.shape[0]):
        hit = jnp.where(row == places[k : k + 1, :], 1.0, hit)
    out_ref[...] = dot_nn(hit.astype(jnp.bfloat16), grad_ref[...]).astype(jnp.bfloat16)


def pick(codes, scales, ids, slots, per_chunk, rows):
    tokens, features = codes.shape
    top = ids.shape[0]
    copies = tokens * top
    whole = lambda shape: pl.BlockSpec(shape, lambda i: (0,) * len(shape))
    tile = ROW_TILE
    return pl.pallas_call(
        functools.partial(pick_kernel, per_chunk, rows),
        grid=(copies // tile,),
        in_specs=[
            whole(codes.shape),
            whole(scales.shape),
            whole(ids.shape),
            whole(slots.shape),
        ],
        out_specs=pl.BlockSpec((tile, features), lambda i: (i, 0)),
        out_shape=jax.ShapeDtypeStruct((copies, features), jnp.bfloat16),
        scratch_shapes=[pltpu.VMEM((tokens, features), jnp.bfloat16)],
        compiler_params=pltpu.CompilerParams(vmem_limit_bytes=VMEM),
        cost_estimate=pl.CostEstimate(
            flops=2 * copies * tokens * features,
            bytes_accessed=2 * features * (copies + tokens),
            transcendentals=0,
        ),
    )(codes, scales, ids, slots)


def expert_kernel(
    rows_ref, gate_own, gate_far, up_own, up_far, dw_own, dw_far, gw_own, gw_far, uw_own, uw_far,
    out_ref,
):
    rows = rows_ref[...]
    total = None
    for gate_ref, up_ref, dw, gw, uw in (
        (gate_own, up_own, dw_own, gw_own, uw_own),
        (gate_far, up_far, dw_far, gw_far, uw_far),
    ):
        hidden = dot_nt(rows, dw[...])
        gate = gate_ref[...].astype(jnp.float32)
        up = up_ref[...].astype(jnp.float32)
        sig = 1.0 / (1.0 + jnp.exp(-gate))
        gate_grad = (hidden * up * sig * (1.0 + gate * (1.0 - sig))).astype(jnp.bfloat16)
        up_grad = (hidden * gate * sig).astype(jnp.bfloat16)
        part = dot_nt(gate_grad, gw[...]) + dot_nt(up_grad, uw[...])
        total = part if total is None else total + part
    out_ref[...] = total.astype(jnp.bfloat16)


def expert(rows, acts, weights):
    count, features = rows.shape
    hidden = acts[0].shape[1]
    tile = ROW_TILE
    by_row = lambda width: pl.BlockSpec((tile, width), lambda i: (i, 0))
    whole = lambda a: pl.BlockSpec(a.shape, lambda i: (0, 0), pipeline_mode=pl.Buffered(1))
    return pl.pallas_call(
        expert_kernel,
        grid=(count // tile,),
        in_specs=[by_row(features)] + [by_row(hidden)] * 4 + [whole(w) for w in weights],
        out_specs=by_row(features),
        out_shape=jax.ShapeDtypeStruct(rows.shape, jnp.bfloat16),
        compiler_params=pltpu.CompilerParams(vmem_limit_bytes=VMEM),
        cost_estimate=pl.CostEstimate(
            flops=2 * 6 * count * features * hidden,
            bytes_accessed=2 * (2 * count * features + 4 * count * hidden + 6 * hidden * features),
            transcendentals=2 * count * hidden,
        ),
    )(rows, *acts, *weights)


def combine_kernel(per_chunk, rows, ids_ref, slots_ref, probs_ref, *refs):
    parts, out_ref = refs[:-1], refs[-1]
    places = place_of(ids_ref, slots_ref, per_chunk, rows)
    tokens = out_ref.shape[0]
    total = None
    for chunk, part_ref in enumerate(parts):
        row = lax.broadcasted_iota(jnp.int32, (rows, tokens), 0) + chunk * rows
        weight = jnp.zeros((rows, tokens), jnp.float32)
        for k in range(places.shape[0]):
            weight = jnp.where(row == places[k : k + 1, :], probs_ref[k : k + 1, :], weight)
        high = weight.astype(jnp.bfloat16)
        low = (weight - high.astype(jnp.float32)).astype(jnp.bfloat16)
        part = part_ref[...]
        term = dot_tn(high, part) + dot_tn(low, part)
        total = term if total is None else total + term
    out_ref[...] = total.astype(jnp.bfloat16)


def combine(ids, slots, probs, parts, tokens, per_chunk):
    rows, features = parts[0].shape
    lanes = features // 7
    whole = lambda a: pl.BlockSpec(a.shape, lambda i: (0, 0))
    return pl.pallas_call(
        functools.partial(combine_kernel, per_chunk, rows),
        grid=(features // lanes,),
        in_specs=[whole(ids), whole(slots), whole(probs)]
        + [pl.BlockSpec((rows, lanes), lambda i: (0, i)) for _ in parts],
        out_specs=pl.BlockSpec((tokens, lanes), lambda i: (0, i)),
        out_shape=jax.ShapeDtypeStruct((tokens, features), jnp.bfloat16),
        compiler_params=pltpu.CompilerParams(vmem_limit_bytes=VMEM),
        cost_estimate=pl.CostEstimate(
            flops=4 * rows * len(parts) * tokens * features,
            bytes_accessed=2 * features * (rows * len(parts) + tokens),
            transcendentals=0,
        ),
    )(ids, slots, probs, *parts)


def shards(
    grad_codes, grad_scales, expert_ids, slots, gate_probs,
    gate_act, up_act, gate_weight, up_weight, down_weight,
):
    token_count, features = grad_codes.shape
    chips = lax.axis_size("row") * lax.axis_size("chip")
    copies = token_count * expert_ids.shape[1]
    per_pair = copies // chips
    per_chunk = per_pair // CHUNKS
    rows = copies // CHUNKS
    hidden = gate_act.shape[2]
    core = lax.axis_index("core")

    ids, slot, probs = expert_ids.T, slots.T, gate_probs.T
    picked = pick(grad_codes, grad_scales, ids, slot, per_chunk, rows)

    exchange = lambda a: lax.all_to_all(a, ("row", "chip"), 0, 0, tiled=True)
    other = lambda a: lax.ppermute(a, "core", SWAP)
    arrived = [
        exchange(picked[c * rows : (c + 1) * rows].reshape(chips, per_chunk, features))
        for c in range(CHUNKS)
    ]
    weights = []
    for w in (down_weight, gate_weight, up_weight):
        weights += [w[0], other(w[0])]
    acts = []
    for act in (gate_act, up_act):
        split = act[0].reshape(chips, GROUP, per_pair, hidden)
        mine = lax.dynamic_index_in_dim(split, core, 1, keepdims=False)
        theirs = lax.dynamic_index_in_dim(split, 1 - core, 1, keepdims=False)
        acts += [mine, other(theirs)]

    returned = []
    for c in range(CHUNKS):
        cut = [
            a[:, c * per_chunk : (c + 1) * per_chunk].reshape(rows, hidden) for a in acts
        ]
        part = expert(arrived[c].reshape(rows, features), cut, weights)
        returned.append(
            exchange(part.reshape(chips, per_chunk, features)).reshape(rows, features)
        )
    return combine(ids, slot, probs, returned, token_count, per_chunk)


def solution(mesh):
    rows, cols = mesh.devices.shape
    fine = Mesh(mesh.devices.reshape(rows, cols // GROUP, GROUP), ("row", "chip", "core"))
    every = ("row", "chip", "core")
    two, three = P(every, None), P(every, None, None)
    return jax.shard_map(
        shards,
        mesh=fine,
        in_specs=(two,) * 5 + (three,) * 5,
        out_specs=two,
        check_vma=False,
    )
```

```python
import functools

import jax
import jax.numpy as jnp
import numpy as np
from jax import lax
from jax.experimental import pallas as pl
from jax.experimental.pallas import tpu as pltpu
from jax.sharding import Mesh
from jax.sharding import PartitionSpec as P

GROUP = 2
SIDE = 4
MEMBERS = 8
META = 128
LANES = 512
EARLY = (0, 7, 6, 1)
LATE = (3, 4, 5, 2)
VMEM = 56 * 1024 * 1024


def place_of_chip(chip):
    return (chip // 8) % SIDE, chip % SIDE, chip // 32 * 2 + chip // 4 % 2


def chip_at(x, y, z):
    return ((z // 2 * SIDE + x) * 2 + z % 2) * SIDE + y


def member_of(chip, kind, member):
    place = []
    for axis, at in enumerate(place_of_chip(chip)):
        bit = member >> (2 - axis) & 1
        place.append(((at + kind) ^ bit) - kind & SIDE - 1)
    return chip_at(*place)


def pairs(devices, swapped, member):
    found = []
    for device in range(devices):
        chip, core = divmod(device, GROUP)
        found.append((device, member_of(chip, core ^ swapped, member) * GROUP + core))
    return found


def tables(devices):
    experts, mine, theirs = [], [], []
    for device in range(devices):
        chip, core = divmod(device, GROUP)
        experts.append([member_of(chip, 1 - core, m) for m in range(MEMBERS)])
        for other, blocks in ((core, mine), (1 - core, theirs)):
            blocks.append(
                [
                    member_of(member_of(chip, 1 - other, m), other, g) * GROUP + other
                    for m in EARLY + LATE
                    for g in range(MEMBERS)
                ]
            )
    return [np.array(t, np.int32) for t in (experts, mine, theirs)]


def dot_nt(left, right):
    return lax.dot_general(
        left, right, (((1,), (1,)), ((), ())), preferred_element_type=jnp.float32
    )


def dot_tn(left, right):
    return lax.dot_general(
        left, right, (((0,), (0,)), ((), ())), preferred_element_type=jnp.float32
    )


def dot_nn(left, right):
    return jnp.dot(left, right, preferred_element_type=jnp.float32)


def cost(flops, moved):
    return pl.CostEstimate(flops=flops, bytes_accessed=moved, transcendentals=0)


def split(value):
    high = value.astype(jnp.bfloat16)
    return high, (value - high.astype(jnp.float32)).astype(jnp.bfloat16)


def pack_kernel(codes_ref, scales_ref, ids_ref, slots_ref, probs_ref, out_ref):
    features = codes_ref.shape[1]
    blocks = scales_ref.shape[0]
    width = features // blocks
    scales = scales_ref[...]
    for start in range(0, features, LANES):
        lane = lax.broadcasted_iota(jnp.int32, (blocks, LANES), 1) + start
        block = lax.broadcasted_iota(jnp.int32, (blocks, LANES), 0)
        spread = jnp.where(lane // width == block, 1.0, 0.0).astype(jnp.bfloat16)
        lanes = slice(start, start + LANES)
        out_ref[:, lanes] = (
            codes_ref[:, lanes].astype(jnp.float32) * dot_tn(scales, spread)
        ).astype(jnp.bfloat16)
    high, low = split(probs_ref[...])
    facts = jnp.concatenate(
        [ids_ref[...].astype(jnp.float32), slots_ref[...].astype(jnp.float32),
         high.astype(jnp.float32), low.astype(jnp.float32)], axis=0,
    ).astype(jnp.bfloat16)
    count = facts.shape[0]
    spread = jnp.where(
        lax.broadcasted_iota(jnp.int32, (count, META), 0)
        == lax.broadcasted_iota(jnp.int32, (count, META), 1), 1.0, 0.0,
    ).astype(jnp.bfloat16)
    out_ref[:, features:] = dot_tn(facts, spread).astype(jnp.bfloat16)


def pack(codes, scales, ids, slots, probs):
    tokens, features = codes.shape
    return pl.pallas_call(
        pack_kernel,
        out_shape=jax.ShapeDtypeStruct((tokens, features + META), jnp.bfloat16),
        compiler_params=pltpu.CompilerParams(vmem_limit_bytes=VMEM),
        cost_estimate=cost(2 * tokens * features * scales.shape[0], 4 * tokens * features),
    )(codes, scales, ids, slots, probs)


def wanted(experts_ref, per_pair, rows):
    lane = lax.broadcasted_iota(jnp.int32, (1, rows), 1)
    message = lane // per_pair
    want = jnp.zeros((1, rows), jnp.int32)
    for m in range(MEMBERS):
        want = jnp.where(message == m, experts_ref[m], want)
    return (want * per_pair + (lane - message * per_pair)).astype(jnp.float32)


def places_in(meta, top, per_pair):
    meta = meta.astype(jnp.float32)
    return meta[:, :top] * float(per_pair) + meta[:, top : 2 * top], meta


def pick_kernel(top, per_pair, experts_ref, *refs):
    metas, grads = refs[:MEMBERS], refs[MEMBERS : 2 * MEMBERS]
    outs, hit_ref = refs[2 * MEMBERS : 3 * MEMBERS], refs[-1]
    rows = MEMBERS * per_pair
    tokens = metas[0].shape[0]

    @pl.when(pl.program_id(0) == 0)
    def _():
        want = wanted(experts_ref, per_pair, rows)
        for g in range(MEMBERS):
            place, _ = places_in(metas[g][...], top, per_pair)
            hit = jnp.zeros((tokens, rows), jnp.float32)
            for k in range(top):
                hit = jnp.where(place[:, k : k + 1] == want, 1.0, hit)
            hit_ref[g] = hit.astype(jnp.bfloat16)

    for g in range(MEMBERS):
        picked = dot_tn(hit_ref[g], grads[g][...]).astype(jnp.bfloat16)
        for m in range(MEMBERS):
            outs[m][g * per_pair : (g + 1) * per_pair, :] = picked[m * per_pair : (m + 1) * per_pair, :]


def pick(experts, gathered, features, top, per_pair):
    tokens = gathered[0].shape[0]
    rows = MEMBERS * per_pair
    meta = pl.BlockSpec((tokens, META), lambda i, *_: (0, features // META))
    tile = pl.BlockSpec((tokens, LANES), lambda i, *_: (0, i))
    out = pl.BlockSpec((rows, LANES), lambda i, *_: (0, i))
    return pl.pallas_call(
        functools.partial(pick_kernel, top, per_pair),
        grid_spec=pltpu.PrefetchScalarGridSpec(
            num_scalar_prefetch=1,
            grid=(features // LANES,),
            in_specs=[meta] * MEMBERS + [tile] * MEMBERS,
            out_specs=[out] * MEMBERS,
            scratch_shapes=[pltpu.VMEM((MEMBERS, tokens, rows), jnp.bfloat16)],
        ),
        out_shape=[jax.ShapeDtypeStruct((rows, features), jnp.bfloat16)] * MEMBERS,
        compiler_params=pltpu.CompilerParams(vmem_limit_bytes=VMEM),
        cost_estimate=cost(
            2 * MEMBERS * rows * tokens * features, 2 * MEMBERS * features * (rows + tokens)
        ),
    )(experts, *gathered, *gathered)


def weigh_kernel(top, per_pair, experts_ref, *refs):
    metas, high_ref, low_ref = refs[:MEMBERS], refs[-2], refs[-1]
    rows = MEMBERS * per_pair
    tokens = metas[0].shape[0]
    want = wanted(experts_ref, per_pair, rows)
    for g in range(MEMBERS):
        place, meta = places_in(metas[g][...], top, per_pair)
        high = jnp.zeros((tokens, rows), jnp.float32)
        low = jnp.zeros((tokens, rows), jnp.float32)
        for k in range(top):
            hit = place[:, k : k + 1] == want
            high = jnp.where(hit, meta[:, 2 * top + k : 2 * top + k + 1], high)
            low = jnp.where(hit, meta[:, 3 * top + k : 3 * top + k + 1], low)
        high_ref[g] = high.astype(jnp.bfloat16)
        low_ref[g] = low.astype(jnp.bfloat16)


def weigh(experts, gathered, features, top, per_pair):
    tokens = gathered[0].shape[0]
    rows = MEMBERS * per_pair
    shape = (MEMBERS, tokens, rows)
    meta = pl.BlockSpec((tokens, META), lambda i, *_: (0, features // META))
    out = pl.BlockSpec(shape, lambda i, *_: (0, 0, 0))
    return pl.pallas_call(
        functools.partial(weigh_kernel, top, per_pair),
        grid_spec=pltpu.PrefetchScalarGridSpec(
            num_scalar_prefetch=1, grid=(1,), in_specs=[meta] * MEMBERS, out_specs=[out, out]
        ),
        out_shape=[jax.ShapeDtypeStruct(shape, jnp.bfloat16)] * 2,
        compiler_params=pltpu.CompilerParams(vmem_limit_bytes=VMEM),
        cost_estimate=cost(0, 1 << 22),
    )(experts, *gathered)


def expert_kernel(first, count, *refs):
    messages, refs = refs[:count], refs[count:]
    acts, weights, outs = refs[:4], refs[4:10], refs[10 : 10 + count]
    rows_ref, act_ref, out_ref, in_sem, act_sem, weight_sem, out_sem = refs[10 + count : 17 + count]
    held = refs[17 + count :]
    size = messages[0].shape[0]
    total, features = rows_ref.shape

    rows_in = [
        pltpu.make_async_copy(ref, rows_ref.at[pl.ds(m * size, size)], in_sem.at[m])
        for m, ref in enumerate(messages)
    ]
    acts_in = [
        pltpu.make_async_copy(ref.at[pl.ds(first, total)], act_ref.at[n], act_sem.at[n])
        for n, ref in enumerate(acts)
    ]
    weights_in = [
        pltpu.make_async_copy(ref, held[n], weight_sem.at[n]) for n, ref in enumerate(weights)
    ]
    for copy in rows_in + weights_in[:1] + acts_in[:2] + weights_in[1:2] + acts_in[2:] + weights_in[2:]:
        copy.start()

    for copy in rows_in:
        copy.wait()
    grads = []
    for half in range(GROUP):
        weights_in[half].wait()
        hidden = dot_nt(rows_ref[...], held[half][...])
        acts_in[2 * half].wait()
        acts_in[2 * half + 1].wait()
        gate = act_ref[2 * half].astype(jnp.float32)
        up = act_ref[2 * half + 1].astype(jnp.float32)
        sig = 1.0 / (1.0 + jnp.exp(-gate))
        grads.append((hidden * up * sig * (1.0 + gate * (1.0 - sig))).astype(jnp.bfloat16))
        grads.append((hidden * gate * sig).astype(jnp.bfloat16))
    for copy in weights_in[2:]:
        copy.wait()

    lanes = features // 2
    copies = []
    for part in range(2):
        here = slice(part * lanes, (part + 1) * lanes)
        for start in range(part * lanes, (part + 1) * lanes, lanes // 7):
            cut = slice(start, start + lanes // 7)
            result = dot_nt(grads[0], held[2][cut, :])
            for n in range(1, 4):
                result = result + dot_nt(grads[n], held[2 + n][cut, :])
            out_ref[:, cut] = result.astype(jnp.bfloat16)
        for m, ref in enumerate(outs):
            copy = pltpu.make_async_copy(
                out_ref.at[pl.ds(m * size, size), here], ref.at[:, here], out_sem.at[part, m]
            )
            copy.start()
            copies.append(copy)
    for copy in copies:
        copy.wait()


def expert(first, messages, acts, weights):
    count = len(messages)
    size, features = messages[0].shape
    rows, hidden = count * size, acts[0].shape[1]
    anywhere = pl.BlockSpec(memory_space=pl.ANY)
    return pl.pallas_call(
        functools.partial(expert_kernel, first, count),
        in_specs=[anywhere] * (count + len(acts) + len(weights)),
        out_specs=[anywhere] * count,
        out_shape=[jax.ShapeDtypeStruct((size, features), jnp.bfloat16)] * count,
        scratch_shapes=[
            pltpu.VMEM((rows, features), jnp.bfloat16),
            pltpu.VMEM((len(acts), rows, hidden), jnp.bfloat16),
            pltpu.VMEM((rows, features), jnp.bfloat16),
            pltpu.SemaphoreType.DMA((count,)),
            pltpu.SemaphoreType.DMA((len(acts),)),
            pltpu.SemaphoreType.DMA((len(weights),)),
            pltpu.SemaphoreType.DMA((2, count)),
        ]
        + [pltpu.VMEM(w.shape, jnp.bfloat16) for w in weights],
        compiler_params=pltpu.CompilerParams(vmem_limit_bytes=VMEM),
        cost_estimate=cost(
            12 * rows * features * hidden,
            4 * rows * features + 8 * rows * hidden + 12 * hidden * features,
        ),
    )(*messages, *acts, *weights)


def combine_kernel(per_pair, high_ref, low_ref, *refs):
    messages, outs = refs[:MEMBERS], refs[MEMBERS:]
    for g in range(MEMBERS):
        rows = jnp.concatenate(
            [message[g * per_pair : (g + 1) * per_pair, :] for message in messages], axis=0
        )
        total = dot_nn(high_ref[g], rows) + dot_nn(low_ref[g], rows)
        outs[g][...] = total.astype(outs[g].dtype)


def combine(high, low, messages, per_pair):
    rows, features = messages[0].shape
    tokens = high.shape[1]
    whole = pl.BlockSpec(high.shape, lambda i: (0, 0, 0))
    tile = pl.BlockSpec((rows, LANES), lambda i: (0, i))
    out = pl.BlockSpec((tokens, LANES), lambda i: (0, i))
    return pl.pallas_call(
        functools.partial(combine_kernel, per_pair),
        grid=(features // LANES,),
        in_specs=[whole, whole] + [tile] * MEMBERS,
        out_specs=[out] * MEMBERS,
        out_shape=[
            jax.ShapeDtypeStruct((tokens, features), jnp.float32 if g == 0 else jnp.bfloat16)
            for g in range(MEMBERS)
        ],
        compiler_params=pltpu.CompilerParams(vmem_limit_bytes=VMEM),
        cost_estimate=cost(
            4 * MEMBERS * rows * tokens * features, 2 * MEMBERS * features * (rows + tokens)
        ),
    )(high, low, *messages)


def shards(
    grad_codes, grad_scales, expert_ids, slots, gate_probs,
    gate_act, up_act, gate_weight, up_weight, down_weight,
):
    token_count, features = grad_codes.shape
    top = expert_ids.shape[1]
    devices = lax.axis_size("i")
    per_pair = token_count * top // (devices // GROUP)
    hidden = gate_act.shape[2]
    device = lax.axis_index("i")
    experts, mine, theirs = (
        lax.dynamic_index_in_dim(jnp.asarray(t), device, 0, keepdims=False)
        for t in tables(devices)
    )

    def within(swapped, member, value):
        return lax.ppermute(value, "i", pairs(devices, swapped, member))

    gather = functools.partial(within, 0)
    exchange = functools.partial(within, 1)

    def other(value):
        return lax.ppermute(value, "i", [(d, d ^ 1) for d in range(devices)])

    packed = pack(grad_codes, grad_scales.T, expert_ids.T, slots.T, gate_probs.T)
    got = {0: packed}
    for member in (7, 4, 2, 1):
        got[member] = gather(member, packed)
    for member, axis, first in ((6, 2, 4), (3, 1, 2), (5, 4, 1)):
        got[member] = gather(axis, got[first])
    gathered = [got[m] for m in range(MEMBERS)]

    acts = [[], []]
    for act in (gate_act, up_act):
        blocks = act[0].reshape(devices, per_pair, hidden)
        own, far = (
            blocks.at[at].get(mode="promise_in_bounds").reshape(-1, hidden) for at in (mine, theirs)
        )
        acts[0].append(own)
        acts[1].append(other(far))
    acts = acts[0] + acts[1]
    down, gate, up = down_weight[0], gate_weight[0], up_weight[0]
    weights = [down, other(down), gate, up, other(gate), other(up)]

    messages = pick(experts, gathered, features, top, per_pair)
    high, low = weigh(experts, gathered, features, top, per_pair)
    arrived = {m: exchange(m, messages[m]) if m else messages[m] for m in EARLY + LATE}
    results = {}
    for first, members in ((0, EARLY), (len(EARLY), LATE)):
        parts = expert(
            first * MEMBERS * per_pair, [arrived[m] for m in members], acts, weights
        )
        for m, part in zip(members, parts):
            results[m] = exchange(m, part) if m else part
    sums = combine(high, low, [results[m] for m in range(MEMBERS)], per_pair)
    total = sums[0]
    for m in range(1, MEMBERS):
        total = total + gather(m, sums[m]).astype(jnp.float32)
    return total.astype(jnp.bfloat16)


def solution(mesh):
    flat = Mesh(mesh.devices.reshape(-1), ("i",))
    two, three = P("i", None), P("i", None, None)
    return jax.shard_map(
        shards, mesh=flat, in_specs=(two,) * 5 + (three,) * 5, out_specs=two, check_vma=False
    )
```

```python
import functools

import jax
import jax.numpy as jnp
from jax import lax
from jax.experimental import pallas as pl
from jax.experimental.pallas import tpu as pltpu
from jax.sharding import Mesh
from jax.sharding import PartitionSpec as P

GROUP = 2
SIDE = 4
MEMBERS = 8
META = 128
LANES = 512
WIDE = 1792
AHEAD = 2
CUTS = ((0, 2048), (2048, 1536))
EARLY = (0, 3, 5, 4, 2)
LATE = (7, 6, 1)
ORDER = EARLY + LATE
VMEM = 62 * 1024 * 1024
EXPERT_VMEM = 40 * 1024 * 1024


def place_of_chip(chip):
    return (chip // 8) % SIDE, chip % SIDE, chip // 32 * 2 + chip // 4 % 2


def chip_at(x, y, z):
    return ((z // 2 * SIDE + x) * 2 + z % 2) * SIDE + y


def member_of(chip, kind, member):
    place = []
    for axis, at in enumerate(place_of_chip(chip)):
        bit = member >> (2 - axis) & 1
        place.append(((at + kind) ^ bit) - kind & SIDE - 1)
    return chip_at(*place)


def pairs(devices, swapped, member):
    found = []
    for device in range(devices):
        chip, core = divmod(device, GROUP)
        found.append((device, member_of(chip, core ^ swapped, member) * GROUP + core))
    return found


def axis_terms(device, swapped, steps):
    chip, core = device // GROUP, lax.rem(device, GROUP) ^ swapped
    places = place_of_chip(chip)
    found = []
    for axis, at in enumerate(places):
        terms = []
        for bits in range(1 << steps):
            here = ((at + (1 - core)) ^ (bits & 1)) - (1 - core) & SIDE - 1
            if steps > 1:
                here = ((here + core) ^ (bits >> 1)) - core & SIDE - 1
            terms.append(chip_at(*[here if n == axis else 0 for n in range(3)]))
        found.append(terms)
    return found


def walk(terms, member, second=0):
    return sum(
        terms[axis][(member >> (2 - axis) & 1) + 2 * (second >> (2 - axis) & 1)] for axis in range(3)
    )


def dot_nt(left, right):
    return lax.dot_general(
        left, right, (((1,), (1,)), ((), ())), preferred_element_type=jnp.float32
    )


def dot_tn(left, right):
    return lax.dot_general(
        left, right, (((0,), (0,)), ((), ())), preferred_element_type=jnp.float32
    )


def dot_nn(left, right):
    return jnp.dot(left, right, preferred_element_type=jnp.float32)


def cost(flops, moved):
    return pl.CostEstimate(flops=flops, bytes_accessed=moved, transcendentals=0)


def split(value):
    high = value.astype(jnp.bfloat16)
    return high, (value - high.astype(jnp.float32)).astype(jnp.bfloat16)


def pack_tokens(codes_ref, scales_ref, ids_ref, slots_ref, probs_ref, out_ref):
    features = codes_ref.shape[1]
    blocks = scales_ref.shape[0]
    width = features // blocks
    scales = scales_ref[...]
    for start in range(0, features, LANES):
        lane = lax.broadcasted_iota(jnp.int32, (blocks, LANES), 1) + start
        block = lax.broadcasted_iota(jnp.int32, (blocks, LANES), 0)
        spread = jnp.where(lane // width == block, 1.0, 0.0).astype(jnp.bfloat16)
        lanes = slice(start, start + LANES)
        out_ref[:, lanes] = (
            codes_ref[:, lanes].astype(jnp.float32) * dot_tn(scales, spread)
        ).astype(jnp.bfloat16)
    high, low = split(probs_ref[...])
    facts = jnp.concatenate(
        [ids_ref[...].astype(jnp.float32), slots_ref[...].astype(jnp.float32),
         high.astype(jnp.float32), low.astype(jnp.float32)], axis=0,
    ).astype(jnp.bfloat16)
    count = facts.shape[0]
    spread = jnp.where(
        lax.broadcasted_iota(jnp.int32, (count, META), 0)
        == lax.broadcasted_iota(jnp.int32, (count, META), 1), 1.0, 0.0,
    ).astype(jnp.bfloat16)
    out_ref[:, features:] = dot_tn(facts, spread).astype(jnp.bfloat16)


def prepare_kernel(per_pair, device_ref, codes, scales, ids, slots, probs, gate_act, up_act, packed, own_out, far_out, own_ref, far_ref, in_sem, out_sem):
    rows = own_ref.shape[0] // 2
    for swapped, part, sem in ((1, far_ref, in_sem.at[1]), (0, own_ref, in_sem.at[0])):
        terms = axis_terms(device_ref[0], swapped, 2)
        core = lax.rem(device_ref[0], GROUP) ^ swapped
        for m, member in enumerate(ORDER):
            for g in range(MEMBERS):
                block = walk(terms, member, g) * GROUP + core
                at = (m * MEMBERS + g) * per_pair
                for n, act in enumerate((gate_act, up_act)):
                    pltpu.make_async_copy(
                        act.at[block], part.at[pl.ds(n * rows + at, per_pair)], sem
                    ).start()
    pack_tokens(codes, scales, ids, slots, probs, packed)
    copies = []
    for n, (part, out) in ((1, (far_ref, far_out)), (0, (own_ref, own_out))):
        pltpu.make_async_copy(part, part, in_sem.at[n]).wait()
        copies.append(pltpu.make_async_copy(part, out, out_sem.at[n]))
        copies[-1].start()
    for copy in copies:
        copy.wait()


def prepare(device, codes, scales, ids, slots, probs, gate_act, up_act):
    tokens, features = codes.shape
    _, per_pair, units = gate_act.shape
    rows = tokens * ids.shape[0]
    anywhere = pl.BlockSpec(memory_space=pl.ANY)
    whole = pl.BlockSpec(memory_space=pltpu.VMEM)
    act = jax.ShapeDtypeStruct((2 * rows, units), jnp.bfloat16)
    return pl.pallas_call(
        functools.partial(prepare_kernel, per_pair),
        in_specs=[pl.BlockSpec(memory_space=pltpu.SMEM)] + [whole] * 5 + [anywhere] * 2,
        out_specs=[whole, anywhere, anywhere],
        out_shape=[jax.ShapeDtypeStruct((tokens, features + META), jnp.bfloat16), act, act],
        scratch_shapes=[pltpu.VMEM(act.shape, jnp.bfloat16)] * 2
        + [pltpu.SemaphoreType.DMA((2,)), pltpu.SemaphoreType.DMA((2,))],
        compiler_params=pltpu.CompilerParams(vmem_limit_bytes=VMEM),
        cost_estimate=cost(2 * tokens * features * scales.shape[0], 4 * tokens * features + 16 * rows * units),
    )(device, codes, scales, ids, slots, probs, gate_act, up_act)


def wanted(device_ref, per_pair, rows):
    lane = lax.broadcasted_iota(jnp.int32, (1, rows), 1)
    message = lane // per_pair
    want = jnp.zeros((1, rows), jnp.int32)
    terms = axis_terms(device_ref[0], 0, 1)
    for m, member in enumerate(ORDER):
        want = jnp.where(message == m, walk(terms, member), want)
    return (want * per_pair + (lane - message * per_pair)).astype(jnp.float32)


def spread_of(meta, column, scale, top, rows):
    lane = lax.broadcasted_iota(jnp.int32, (META, top * rows), 1) // rows
    line = lax.broadcasted_iota(jnp.int32, (META, top * rows), 0)
    chosen = jnp.zeros((META, top * rows), jnp.float32)
    for first, factor in zip(column, scale):
        chosen = jnp.where(line == lane + first, factor, chosen)
    return dot_nn(meta, chosen.astype(jnp.bfloat16))


def pick_kernel(top, per_pair, device_ref, *refs):
    metas, grads = refs[:MEMBERS], refs[MEMBERS : 2 * MEMBERS]
    outs, hit_ref = refs[2 * MEMBERS : 3 * MEMBERS], refs[-1]
    rows = MEMBERS * per_pair

    @pl.when(pl.program_id(0) == 0)
    def _():
        want = wanted(device_ref, per_pair, rows)
        for g in range(MEMBERS):
            place = spread_of(metas[g][...], (0, top), (float(per_pair), 1.0), top, rows)
            hit = jnp.zeros((place.shape[0], rows), jnp.float32)
            for k in range(top):
                hit = jnp.where(place[:, k * rows : (k + 1) * rows] == want, 1.0, hit)
            hit_ref[g] = hit.T.astype(jnp.bfloat16)

    for g in range(MEMBERS):
        picked = dot_nn(hit_ref[g], grads[g][...]).astype(jnp.bfloat16)
        for m in range(MEMBERS):
            outs[m][g * per_pair : (g + 1) * per_pair, :] = picked[m * per_pair : (m + 1) * per_pair, :]


def pick(device, gathered, features, top, per_pair):
    tokens = gathered[0].shape[0]
    rows = MEMBERS * per_pair
    meta = pl.BlockSpec((tokens, META), lambda i, *_: (0, features // META))
    tile = pl.BlockSpec((tokens, WIDE), lambda i, *_: (0, i))
    out = pl.BlockSpec((rows, WIDE), lambda i, *_: (0, i))
    return pl.pallas_call(
        functools.partial(pick_kernel, top, per_pair),
        grid_spec=pltpu.PrefetchScalarGridSpec(
            num_scalar_prefetch=1,
            grid=(features // WIDE,),
            in_specs=[meta] * MEMBERS + [tile] * MEMBERS,
            out_specs=[out] * MEMBERS,
            scratch_shapes=[pltpu.VMEM((MEMBERS, rows, tokens), jnp.bfloat16)],
        ),
        out_shape=[jax.ShapeDtypeStruct((rows, features), jnp.bfloat16)] * MEMBERS,
        compiler_params=pltpu.CompilerParams(vmem_limit_bytes=VMEM),
        cost_estimate=cost(
            2 * MEMBERS * rows * tokens * features, 2 * MEMBERS * features * (rows + tokens)
        ),
    )(device, *gathered, *gathered)


def weigh_kernel(top, per_pair, device_ref, *refs):
    metas, high_ref, low_ref = refs[:MEMBERS], refs[-2], refs[-1]
    rows = MEMBERS * per_pair
    want = wanted(device_ref, per_pair, rows)
    for g in range(MEMBERS):
        meta = metas[g][...]
        place = spread_of(meta, (0, top), (float(per_pair), 1.0), top, rows)
        highs = spread_of(meta, (2 * top,), (1.0,), top, rows)
        lows = spread_of(meta, (3 * top,), (1.0,), top, rows)
        high = jnp.zeros((place.shape[0], rows), jnp.float32)
        low = jnp.zeros((place.shape[0], rows), jnp.float32)
        for k in range(top):
            lanes = slice(k * rows, (k + 1) * rows)
            hit = place[:, lanes] == want
            high = jnp.where(hit, highs[:, lanes], high)
            low = jnp.where(hit, lows[:, lanes], low)
        high_ref[g] = high.astype(jnp.bfloat16)
        low_ref[g] = low.astype(jnp.bfloat16)


def weigh(device, gathered, features, top, per_pair):
    tokens = gathered[0].shape[0]
    rows = MEMBERS * per_pair
    shape = (MEMBERS, tokens, rows)
    meta = pl.BlockSpec((tokens, META), lambda i, *_: (0, features // META))
    out = pl.BlockSpec(shape, lambda i, *_: (0, 0, 0))
    return pl.pallas_call(
        functools.partial(weigh_kernel, top, per_pair),
        grid_spec=pltpu.PrefetchScalarGridSpec(
            num_scalar_prefetch=1, grid=(1,), in_specs=[meta] * MEMBERS, out_specs=[out, out]
        ),
        out_shape=[jax.ShapeDtypeStruct(shape, jnp.bfloat16)] * 2,
        compiler_params=pltpu.CompilerParams(vmem_limit_bytes=VMEM),
        cost_estimate=cost(0, 1 << 22),
    )(device, *gathered)


def expert_kernel(first, count, *refs):
    messages, refs = refs[:count], refs[count:]
    own_acts, far_acts, down, back, refs = *refs[:2], refs[2:4], refs[4:8], refs[8:]
    outs, (rows_ref, act_ref, down_ref, back_ref, grad_ref) = refs[:count], refs[count : count + 5]
    in_sem, act_sem, down_sem, back_sem, out_sem = refs[count + 5 :]
    size = messages[0].shape[0]
    total, features = rows_ref.shape
    units = act_ref.shape[2]
    all_rows = own_acts.shape[0] // 2

    cuts = [pl.ds(*cut) for cut in CUTS]
    rows_in = [
        [
            pltpu.make_async_copy(
                ref.at[:, cut], rows_ref.at[pl.ds(m * size, size), cut], in_sem.at[c, m]
            )
            for m, ref in enumerate(messages)
        ]
        for c, cut in enumerate(cuts)
    ]
    acts_in = [
        pltpu.make_async_copy(
            ref.at[pl.ds(start + first, total)], act_ref.at[n], act_sem.at[n]
        )
        for n, (ref, start) in enumerate(
            ((own_acts, 0), (own_acts, all_rows), (far_acts, 0), (far_acts, all_rows))
        )
    ]
    down_in = [
        [
            pltpu.make_async_copy(
                ref.at[:, cut], down_ref.at[n, :, cut], down_sem.at[n, c]
            )
            for c, cut in enumerate(cuts)
        ]
        for n, ref in enumerate(down)
    ]
    back_in = [
        [
            pltpu.make_async_copy(
                ref.at[pl.ds(start, LANES)],
                back_ref.at[pl.ds(start, LANES), pl.ds(n * units, units)],
                back_sem.at[start // LANES, n],
            )
            for n, ref in enumerate(back)
        ]
        for start in range(0, features, LANES)
    ]
    for c in range(len(cuts)):
        for copy in rows_in[c] + [down_in[0][c]]:
            copy.start()
    for copy in acts_in[:2] + down_in[1] + acts_in[2:]:
        copy.start()
    for tile in back_in[:AHEAD]:
        for copy in tile:
            copy.start()

    for half in range(GROUP):
        hidden = None
        for c, cut in enumerate(cuts):
            for copy in (rows_in[c] if half == 0 else []) + [down_in[half][c]]:
                copy.wait()
            here = slice(CUTS[c][0], sum(CUTS[c]))
            term = dot_nt(rows_ref[:, here], down_ref[half, :, here])
            hidden = term if hidden is None else hidden + term
        acts_in[2 * half].wait()
        acts_in[2 * half + 1].wait()
        gate_pre = act_ref[2 * half].astype(jnp.float32)
        up_pre = act_ref[2 * half + 1].astype(jnp.float32)
        sig = 1.0 / (1.0 + jnp.exp(-gate_pre))
        here = 2 * half * units
        grad_ref[:, here : here + units] = (
            hidden * up_pre * sig * (1.0 + gate_pre * (1.0 - sig))
        ).astype(jnp.bfloat16)
        grad_ref[:, here + units : here + 2 * units] = (hidden * gate_pre * sig).astype(jnp.bfloat16)

    copies = []
    for part, tile in enumerate(back_in):
        for copy in tile:
            copy.wait()
        for later in back_in[part + AHEAD : part + AHEAD + 1]:
            for copy in later:
                copy.start()
        here = slice(part * LANES, (part + 1) * LANES)
        rows_ref[:, here] = dot_nt(grad_ref[...], back_ref[here, :]).astype(jnp.bfloat16)
        for m, ref in enumerate(outs):
            copy = pltpu.make_async_copy(
                rows_ref.at[pl.ds(m * size, size), here], ref.at[:, here], out_sem.at[part, m]
            )
            copy.start()
            copies.append(copy)
    for copy in copies:
        copy.wait()


def expert(first, messages, own_acts, far_acts, *weights):
    count = len(messages)
    size, features = messages[0].shape
    rows, units = count * size, own_acts.shape[1]
    tiles = features // LANES
    anywhere = pl.BlockSpec(memory_space=pl.ANY)
    return pl.pallas_call(
        functools.partial(expert_kernel, first, count),
        in_specs=[anywhere] * (count + 2 + len(weights)),
        out_specs=[anywhere] * count,
        out_shape=[jax.ShapeDtypeStruct((size, features), jnp.bfloat16)] * count,
        scratch_shapes=[
            pltpu.VMEM((rows, features), jnp.bfloat16),
            pltpu.VMEM((2 * GROUP, rows, units), jnp.bfloat16),
            pltpu.VMEM((GROUP, units, features), jnp.bfloat16),
            pltpu.VMEM((features, 2 * GROUP * units), jnp.bfloat16),
            pltpu.VMEM((rows, 2 * GROUP * units), jnp.bfloat16),
            pltpu.SemaphoreType.DMA((len(CUTS), count)),
            pltpu.SemaphoreType.DMA((2 * GROUP,)),
            pltpu.SemaphoreType.DMA((GROUP, len(CUTS))),
            pltpu.SemaphoreType.DMA((tiles, 2 * GROUP)),
            pltpu.SemaphoreType.DMA((tiles, count)),
        ],
        compiler_params=pltpu.CompilerParams(vmem_limit_bytes=EXPERT_VMEM),
        cost_estimate=cost(
            12 * rows * features * units,
            4 * rows * features + 8 * rows * units + 12 * units * features,
        ),
    )(*messages, own_acts, far_acts, *weights)


def combine_kernel(per_pair, high_ref, low_ref, *refs):
    messages, outs = refs[:MEMBERS], refs[MEMBERS:]
    for g in range(MEMBERS):
        rows = jnp.concatenate(
            [message[g * per_pair : (g + 1) * per_pair, :] for message in messages], axis=0
        )
        total = dot_nn(high_ref[g], rows) + dot_nn(low_ref[g], rows)
        outs[g][...] = total.astype(outs[g].dtype)


def combine(high, low, messages, per_pair):
    rows, features = messages[0].shape
    tokens = high.shape[1]
    whole = pl.BlockSpec(high.shape, lambda i: (0, 0, 0))
    tile = pl.BlockSpec((rows, WIDE), lambda i: (0, i))
    out = pl.BlockSpec((tokens, WIDE), lambda i: (0, i))
    return pl.pallas_call(
        functools.partial(combine_kernel, per_pair),
        grid=(features // WIDE,),
        in_specs=[whole, whole] + [tile] * MEMBERS,
        out_specs=[out] * MEMBERS,
        out_shape=[
            jax.ShapeDtypeStruct((tokens, features), jnp.float32 if g == 0 else jnp.bfloat16)
            for g in range(MEMBERS)
        ],
        compiler_params=pltpu.CompilerParams(vmem_limit_bytes=36 * 1024 * 1024),
        cost_estimate=cost(
            4 * MEMBERS * rows * tokens * features, 2 * MEMBERS * features * (rows + tokens)
        ),
    )(high, low, *messages)


def shards(
    grad_codes, grad_scales, expert_ids, slots, gate_probs,
    gate_act, up_act, gate_weight, up_weight, down_weight,
):
    token_count, features = grad_codes.shape
    top = expert_ids.shape[1]
    devices = lax.axis_size("i")
    per_pair = token_count * top // (devices // GROUP)
    hidden = gate_act.shape[2]
    device = lax.axis_index("i").reshape(1)

    def within(swapped, member, value):
        return lax.ppermute(value, "i", pairs(devices, swapped, member))

    gather = functools.partial(within, 0)
    exchange = functools.partial(within, 1)

    def other(value):
        return lax.ppermute(value, "i", [(d, d ^ 1) for d in range(devices)])

    blocks = (devices, per_pair, hidden)
    packed, own_acts, far_acts = prepare(
        device, grad_codes, grad_scales.T, expert_ids.T, slots.T, gate_probs.T,
        gate_act.reshape(blocks), up_act.reshape(blocks),
    )
    own = [down_weight[0], gate_weight[0], up_weight[0]]
    far = [other(w) for w in own]
    got = {0: packed, 4: gather(4, packed), 2: gather(2, packed)}
    next_packed, far[0] = lax.optimization_barrier((packed, far[0]))
    got[1] = gather(1, next_packed)
    next_packed, far[1] = lax.optimization_barrier((next_packed, far[1]))
    got[7] = gather(7, next_packed)
    far_acts, far[2] = lax.optimization_barrier((far_acts, far[2]))
    far_acts = other(far_acts)
    weights = [own[0], far[0], own[1], own[2], far[1], far[2]]
    for member, axis, first in ((6, 2, 4), (3, 1, 2), (5, 4, 1)):
        got[member] = gather(axis, got[first])
    gathered = [got[m] for m in range(MEMBERS)]

    messages = dict(zip(ORDER, pick(device, gathered, features, top, per_pair)))
    high, low = weigh(device, gathered, features, top, per_pair)

    def send(members, parts):
        return [exchange(m, part) if m else part for m, part in zip(members, parts)]

    early = send(EARLY, [messages[m] for m in EARLY])
    late, early[-1], far_acts = lax.optimization_barrier(
        ([messages[m] for m in LATE], early[-1], far_acts)
    )
    late = send(LATE, late)
    held = (own_acts, far_acts, *weights)
    early = expert(0, early, *held)
    late = expert(len(EARLY) * MEMBERS * per_pair, late, *held)
    early = send(EARLY, early)
    late = list(late)
    early[1], late[1:] = lax.optimization_barrier((early[1], late[1:]))
    late = send(LATE, late)
    sums = combine(high, low, early + late, per_pair)
    far = gather(7, sums[7]).astype(jnp.float32)
    total = sums[0]
    for member, axis, first in ((6, 2, 4), (3, 1, 2), (5, 4, 1)):
        passed = sums[first].astype(jnp.float32) + gather(axis, sums[member]).astype(jnp.float32)
        total = total + gather(first, passed.astype(jnp.bfloat16)).astype(jnp.float32)
    return (total + far).astype(jnp.bfloat16)


def solution(mesh):
    flat = Mesh(mesh.devices.reshape(-1), ("i",))
    two, three = P("i", None), P("i", None, None)
    return jax.shard_map(
        shards, mesh=flat, in_specs=(two,) * 5 + (three,) * 5, out_specs=two, check_vma=False
    )
```

```python
import functools

import jax
import jax.numpy as jnp
from jax import lax
from jax.experimental import pallas as pl
from jax.experimental.pallas import tpu as pltpu
from jax.sharding import Mesh
from jax.sharding import PartitionSpec as P

GROUP = 2
SIDE = 4
MEMBERS = 8
META = 128
LANES = 512
WIDE = 1792
AHEAD = 2
CUTS = ((0, 2048), (2048, 1536))
EARLY = (0, 3, 5, 4, 2)
LATE = (7, 6, 1)
ORDER = EARLY + LATE
VMEM = 62 * 1024 * 1024
EXPERT_VMEM = 40 * 1024 * 1024


def place_of_chip(chip):
    return (chip // 8) % SIDE, chip % SIDE, chip // 32 * 2 + chip // 4 % 2


def chip_at(x, y, z):
    return ((z // 2 * SIDE + x) * 2 + z % 2) * SIDE + y


def member_of(chip, kind, member):
    place = []
    for axis, at in enumerate(place_of_chip(chip)):
        bit = member >> (2 - axis) & 1
        place.append(((at + kind) ^ bit) - kind & SIDE - 1)
    return chip_at(*place)


def pairs(devices, swapped, member):
    found = []
    for device in range(devices):
        chip, core = divmod(device, GROUP)
        found.append((device, member_of(chip, core ^ swapped, member) * GROUP + core))
    return found


def axis_terms(device, swapped, steps):
    chip, core = device // GROUP, lax.rem(device, GROUP) ^ swapped
    places = place_of_chip(chip)
    found = []
    for axis, at in enumerate(places):
        terms = []
        for bits in range(1 << steps):
            here = ((at + (1 - core)) ^ (bits & 1)) - (1 - core) & SIDE - 1
            if steps > 1:
                here = ((here + core) ^ (bits >> 1)) - core & SIDE - 1
            terms.append(chip_at(*[here if n == axis else 0 for n in range(3)]))
        found.append(terms)
    return found


def walk(terms, member, second=0):
    return sum(
        terms[axis][(member >> (2 - axis) & 1) + 2 * (second >> (2 - axis) & 1)] for axis in range(3)
    )


def dot_nt(left, right):
    return lax.dot_general(
        left, right, (((1,), (1,)), ((), ())), preferred_element_type=jnp.float32
    )


def dot_tn(left, right):
    return lax.dot_general(
        left, right, (((0,), (0,)), ((), ())), preferred_element_type=jnp.float32
    )


def dot_nn(left, right):
    return jnp.dot(left, right, preferred_element_type=jnp.float32)


def cost(flops, moved):
    return pl.CostEstimate(flops=flops, bytes_accessed=moved, transcendentals=0)


def split(value):
    high = value.astype(jnp.bfloat16)
    return high, (value - high.astype(jnp.float32)).astype(jnp.bfloat16)


def pack_tokens(codes_ref, scales_ref, ids_ref, slots_ref, probs_ref, out_ref):
    features = codes_ref.shape[1]
    blocks = scales_ref.shape[0]
    width = features // blocks
    scales = scales_ref[...]
    for start in range(0, features, LANES):
        lane = lax.broadcasted_iota(jnp.int32, (blocks, LANES), 1) + start
        block = lax.broadcasted_iota(jnp.int32, (blocks, LANES), 0)
        spread = jnp.where(lane // width == block, 1.0, 0.0).astype(jnp.bfloat16)
        lanes = slice(start, start + LANES)
        out_ref[:, lanes] = (
            codes_ref[:, lanes].astype(jnp.float32) * dot_tn(scales, spread)
        ).astype(jnp.bfloat16)
    high, low = split(probs_ref[...])
    facts = jnp.concatenate(
        [ids_ref[...].astype(jnp.float32), slots_ref[...].astype(jnp.float32),
         high.astype(jnp.float32), low.astype(jnp.float32)], axis=0,
    ).astype(jnp.bfloat16)
    count = facts.shape[0]
    spread = jnp.where(
        lax.broadcasted_iota(jnp.int32, (count, META), 0)
        == lax.broadcasted_iota(jnp.int32, (count, META), 1), 1.0, 0.0,
    ).astype(jnp.bfloat16)
    out_ref[:, features:] = dot_tn(facts, spread).astype(jnp.bfloat16)


def pack(codes, scales, ids, slots, probs):
    tokens, features = codes.shape
    return pl.pallas_call(
        pack_tokens,
        out_shape=jax.ShapeDtypeStruct((tokens, features + META), jnp.bfloat16),
        compiler_params=pltpu.CompilerParams(vmem_limit_bytes=VMEM),
        cost_estimate=cost(2 * tokens * features * scales.shape[0], 4 * tokens * features),
    )(codes, scales, ids, slots, probs)


def lay_kernel(per_pair, device_ref, gate_act, up_act, own_out, far_out, own_ref, far_ref, in_sem, out_sem):
    rows = own_ref.shape[0] // 2
    for swapped, part, sem in ((1, far_ref, in_sem.at[1]), (0, own_ref, in_sem.at[0])):
        terms = axis_terms(device_ref[0], swapped, 2)
        core = lax.rem(device_ref[0], GROUP) ^ swapped
        for m, member in enumerate(ORDER):
            for g in range(MEMBERS):
                block = walk(terms, member, g) * GROUP + core
                at = (m * MEMBERS + g) * per_pair
                for n, act in enumerate((gate_act, up_act)):
                    pltpu.make_async_copy(
                        act.at[block], part.at[pl.ds(n * rows + at, per_pair)], sem
                    ).start()
    copies = []
    for n, (part, out) in ((1, (far_ref, far_out)), (0, (own_ref, own_out))):
        pltpu.make_async_copy(part, part, in_sem.at[n]).wait()
        copies.append(pltpu.make_async_copy(part, out, out_sem.at[n]))
        copies[-1].start()
    for copy in copies:
        copy.wait()


def lay(device, gate_act, up_act, rows):
    _, per_pair, units = gate_act.shape
    anywhere = pl.BlockSpec(memory_space=pl.ANY)
    act = jax.ShapeDtypeStruct((2 * rows, units), jnp.bfloat16)
    return pl.pallas_call(
        functools.partial(lay_kernel, per_pair),
        in_specs=[pl.BlockSpec(memory_space=pltpu.SMEM)] + [anywhere] * 2,
        out_specs=[anywhere, anywhere],
        out_shape=[act, act],
        scratch_shapes=[pltpu.VMEM(act.shape, jnp.bfloat16)] * 2
        + [pltpu.SemaphoreType.DMA((2,)), pltpu.SemaphoreType.DMA((2,))],
        compiler_params=pltpu.CompilerParams(vmem_limit_bytes=VMEM),
        cost_estimate=cost(0, 16 * rows * units),
    )(device, gate_act, up_act)


def wanted(device_ref, per_pair, rows):
    lane = lax.broadcasted_iota(jnp.int32, (1, rows), 1)
    message = lane // per_pair
    want = jnp.zeros((1, rows), jnp.int32)
    terms = axis_terms(device_ref[0], 0, 1)
    for m, member in enumerate(ORDER):
        want = jnp.where(message == m, walk(terms, member), want)
    return (want * per_pair + (lane - message * per_pair)).astype(jnp.float32)


def spread_of(meta, column, scale, top, rows):
    lane = lax.broadcasted_iota(jnp.int32, (META, top * rows), 1) // rows
    line = lax.broadcasted_iota(jnp.int32, (META, top * rows), 0)
    chosen = jnp.zeros((META, top * rows), jnp.float32)
    for first, factor in zip(column, scale):
        chosen = jnp.where(line == lane + first, factor, chosen)
    return dot_nn(meta, chosen.astype(jnp.bfloat16))


def pick_kernel(top, per_pair, device_ref, *refs):
    metas, grads = refs[:MEMBERS], refs[MEMBERS : 2 * MEMBERS]
    outs, hit_ref = refs[2 * MEMBERS : 3 * MEMBERS], refs[-1]
    rows = MEMBERS * per_pair

    @pl.when(pl.program_id(0) == 0)
    def _():
        want = wanted(device_ref, per_pair, rows)
        for g in range(MEMBERS):
            place = spread_of(metas[g][...], (0, top), (float(per_pair), 1.0), top, rows)
            hit = jnp.zeros((place.shape[0], rows), jnp.float32)
            for k in range(top):
                hit = jnp.where(place[:, k * rows : (k + 1) * rows] == want, 1.0, hit)
            hit_ref[g] = hit.T.astype(jnp.bfloat16)

    for g in range(MEMBERS):
        picked = dot_nn(hit_ref[g], grads[g][...]).astype(jnp.bfloat16)
        for m in range(MEMBERS):
            outs[m][g * per_pair : (g + 1) * per_pair, :] = picked[m * per_pair : (m + 1) * per_pair, :]


def pick(device, gathered, features, top, per_pair):
    tokens = gathered[0].shape[0]
    rows = MEMBERS * per_pair
    meta = pl.BlockSpec((tokens, META), lambda i, *_: (0, features // META))
    tile = pl.BlockSpec((tokens, WIDE), lambda i, *_: (0, i))
    out = pl.BlockSpec((rows, WIDE), lambda i, *_: (0, i))
    return pl.pallas_call(
        functools.partial(pick_kernel, top, per_pair),
        grid_spec=pltpu.PrefetchScalarGridSpec(
            num_scalar_prefetch=1,
            grid=(features // WIDE,),
            in_specs=[meta] * MEMBERS + [tile] * MEMBERS,
            out_specs=[out] * MEMBERS,
            scratch_shapes=[pltpu.VMEM((MEMBERS, rows, tokens), jnp.bfloat16)],
        ),
        out_shape=[jax.ShapeDtypeStruct((rows, features), jnp.bfloat16)] * MEMBERS,
        compiler_params=pltpu.CompilerParams(vmem_limit_bytes=VMEM),
        cost_estimate=cost(
            2 * MEMBERS * rows * tokens * features, 2 * MEMBERS * features * (rows + tokens)
        ),
    )(device, *gathered, *gathered)


def weigh_kernel(top, per_pair, device_ref, *refs):
    metas, high_ref, low_ref = refs[:MEMBERS], refs[-2], refs[-1]
    rows = MEMBERS * per_pair
    want = wanted(device_ref, per_pair, rows)
    for g in range(MEMBERS):
        meta = metas[g][...]
        place = spread_of(meta, (0, top), (float(per_pair), 1.0), top, rows)
        highs = spread_of(meta, (2 * top,), (1.0,), top, rows)
        lows = spread_of(meta, (3 * top,), (1.0,), top, rows)
        high = jnp.zeros((place.shape[0], rows), jnp.float32)
        low = jnp.zeros((place.shape[0], rows), jnp.float32)
        for k in range(top):
            lanes = slice(k * rows, (k + 1) * rows)
            hit = place[:, lanes] == want
            high = jnp.where(hit, highs[:, lanes], high)
            low = jnp.where(hit, lows[:, lanes], low)
        high_ref[g] = high.astype(jnp.bfloat16)
        low_ref[g] = low.astype(jnp.bfloat16)


def weigh(device, gathered, features, top, per_pair):
    tokens = gathered[0].shape[0]
    rows = MEMBERS * per_pair
    shape = (MEMBERS, tokens, rows)
    meta = pl.BlockSpec((tokens, META), lambda i, *_: (0, features // META))
    out = pl.BlockSpec(shape, lambda i, *_: (0, 0, 0))
    return pl.pallas_call(
        functools.partial(weigh_kernel, top, per_pair),
        grid_spec=pltpu.PrefetchScalarGridSpec(
            num_scalar_prefetch=1, grid=(1,), in_specs=[meta] * MEMBERS, out_specs=[out, out]
        ),
        out_shape=[jax.ShapeDtypeStruct(shape, jnp.bfloat16)] * 2,
        compiler_params=pltpu.CompilerParams(vmem_limit_bytes=VMEM),
        cost_estimate=cost(0, 1 << 22),
    )(device, *gathered)


def expert_kernel(first, count, *refs):
    messages, refs = refs[:count], refs[count:]
    own_acts, far_acts, down, back, refs = *refs[:2], refs[2:4], refs[4:8], refs[8:]
    outs, (rows_ref, act_ref, down_ref, back_ref, grad_ref) = refs[:count], refs[count : count + 5]
    in_sem, act_sem, down_sem, back_sem, out_sem = refs[count + 5 :]
    size = messages[0].shape[0]
    total, features = rows_ref.shape
    units = act_ref.shape[2]
    all_rows = own_acts.shape[0] // 2

    cuts = [pl.ds(*cut) for cut in CUTS]
    rows_in = [
        [
            pltpu.make_async_copy(
                ref.at[:, cut], rows_ref.at[pl.ds(m * size, size), cut], in_sem.at[c, m]
            )
            for m, ref in enumerate(messages)
        ]
        for c, cut in enumerate(cuts)
    ]
    acts_in = [
        pltpu.make_async_copy(
            ref.at[pl.ds(start + first, total)], act_ref.at[n], act_sem.at[n]
        )
        for n, (ref, start) in enumerate(
            ((own_acts, 0), (own_acts, all_rows), (far_acts, 0), (far_acts, all_rows))
        )
    ]
    down_in = [
        [
            pltpu.make_async_copy(
                ref.at[:, cut], down_ref.at[n, :, cut], down_sem.at[n, c]
            )
            for c, cut in enumerate(cuts)
        ]
        for n, ref in enumerate(down)
    ]
    back_in = [
        [
            pltpu.make_async_copy(
                ref.at[pl.ds(start, LANES)],
                back_ref.at[pl.ds(start, LANES), pl.ds(n * units, units)],
                back_sem.at[start // LANES, n],
            )
            for n, ref in enumerate(back)
        ]
        for start in range(0, features, LANES)
    ]
    for c in range(len(cuts)):
        for copy in rows_in[c] + [down_in[0][c]]:
            copy.start()
    for copy in acts_in[:2] + down_in[1] + acts_in[2:]:
        copy.start()
    for tile in back_in[:AHEAD]:
        for copy in tile:
            copy.start()

    for half in range(GROUP):
        hidden = None
        for c, cut in enumerate(cuts):
            for copy in (rows_in[c] if half == 0 else []) + [down_in[half][c]]:
                copy.wait()
            here = slice(CUTS[c][0], sum(CUTS[c]))
            term = dot_nt(rows_ref[:, here], down_ref[half, :, here])
            hidden = term if hidden is None else hidden + term
        acts_in[2 * half].wait()
        acts_in[2 * half + 1].wait()
        gate_pre = act_ref[2 * half].astype(jnp.float32)
        up_pre = act_ref[2 * half + 1].astype(jnp.float32)
        sig = 1.0 / (1.0 + jnp.exp(-gate_pre))
        here = 2 * half * units
        grad_ref[:, here : here + units] = (
            hidden * up_pre * sig * (1.0 + gate_pre * (1.0 - sig))
        ).astype(jnp.bfloat16)
        grad_ref[:, here + units : here + 2 * units] = (hidden * gate_pre * sig).astype(jnp.bfloat16)

    copies = []
    for part, tile in enumerate(back_in):
        for copy in tile:
            copy.wait()
        for later in back_in[part + AHEAD : part + AHEAD + 1]:
            for copy in later:
                copy.start()
        here = slice(part * LANES, (part + 1) * LANES)
        rows_ref[:, here] = dot_nt(grad_ref[...], back_ref[here, :]).astype(jnp.bfloat16)
        for m, ref in enumerate(outs):
            copy = pltpu.make_async_copy(
                rows_ref.at[pl.ds(m * size, size), here], ref.at[:, here], out_sem.at[part, m]
            )
            copy.start()
            copies.append(copy)
    for copy in copies:
        copy.wait()


def expert(first, messages, own_acts, far_acts, *weights):
    count = len(messages)
    size, features = messages[0].shape
    rows, units = count * size, own_acts.shape[1]
    tiles = features // LANES
    anywhere = pl.BlockSpec(memory_space=pl.ANY)
    return pl.pallas_call(
        functools.partial(expert_kernel, first, count),
        in_specs=[anywhere] * (count + 2 + len(weights)),
        out_specs=[anywhere] * count,
        out_shape=[jax.ShapeDtypeStruct((size, features), jnp.bfloat16)] * count,
        scratch_shapes=[
            pltpu.VMEM((rows, features), jnp.bfloat16),
            pltpu.VMEM((2 * GROUP, rows, units), jnp.bfloat16),
            pltpu.VMEM((GROUP, units, features), jnp.bfloat16),
            pltpu.VMEM((features, 2 * GROUP * units), jnp.bfloat16),
            pltpu.VMEM((rows, 2 * GROUP * units), jnp.bfloat16),
            pltpu.SemaphoreType.DMA((len(CUTS), count)),
            pltpu.SemaphoreType.DMA((2 * GROUP,)),
            pltpu.SemaphoreType.DMA((GROUP, len(CUTS))),
            pltpu.SemaphoreType.DMA((tiles, 2 * GROUP)),
            pltpu.SemaphoreType.DMA((tiles, count)),
        ],
        compiler_params=pltpu.CompilerParams(vmem_limit_bytes=EXPERT_VMEM),
        cost_estimate=cost(
            12 * rows * features * units,
            4 * rows * features + 8 * rows * units + 12 * units * features,
        ),
    )(*messages, own_acts, far_acts, *weights)


def combine_kernel(per_pair, high_ref, low_ref, *refs):
    messages, outs = refs[:MEMBERS], refs[MEMBERS:]
    for g in range(MEMBERS):
        rows = jnp.concatenate(
            [message[g * per_pair : (g + 1) * per_pair, :] for message in messages], axis=0
        )
        total = dot_nn(high_ref[g], rows) + dot_nn(low_ref[g], rows)
        outs[g][...] = total.astype(outs[g].dtype)


def combine(high, low, messages, per_pair):
    rows, features = messages[0].shape
    tokens = high.shape[1]
    whole = pl.BlockSpec(high.shape, lambda i: (0, 0, 0))
    tile = pl.BlockSpec((rows, WIDE), lambda i: (0, i))
    out = pl.BlockSpec((tokens, WIDE), lambda i: (0, i))
    return pl.pallas_call(
        functools.partial(combine_kernel, per_pair),
        grid=(features // WIDE,),
        in_specs=[whole, whole] + [tile] * MEMBERS,
        out_specs=[out] * MEMBERS,
        out_shape=[
            jax.ShapeDtypeStruct((tokens, features), jnp.float32 if g == 0 else jnp.bfloat16)
            for g in range(MEMBERS)
        ],
        compiler_params=pltpu.CompilerParams(vmem_limit_bytes=36 * 1024 * 1024),
        cost_estimate=cost(
            4 * MEMBERS * rows * tokens * features, 2 * MEMBERS * features * (rows + tokens)
        ),
    )(high, low, *messages)


def shards(
    grad_codes, grad_scales, expert_ids, slots, gate_probs,
    gate_act, up_act, gate_weight, up_weight, down_weight,
):
    token_count, features = grad_codes.shape
    top = expert_ids.shape[1]
    devices = lax.axis_size("i")
    per_pair = token_count * top // (devices // GROUP)
    hidden = gate_act.shape[2]
    device = lax.axis_index("i").reshape(1)

    def within(swapped, member, value):
        return lax.ppermute(value, "i", pairs(devices, swapped, member))

    gather = functools.partial(within, 0)
    exchange = functools.partial(within, 1)

    def other(value):
        return lax.ppermute(value, "i", [(d, d ^ 1) for d in range(devices)])

    blocks = (devices, per_pair, hidden)
    packed = pack(grad_codes, grad_scales.T, expert_ids.T, slots.T, gate_probs.T)
    own = [down_weight[0], gate_weight[0], up_weight[0]]
    far = [other(w) for w in own]
    got = {0: packed, 4: gather(4, packed), 2: gather(2, packed)}
    next_packed, far[0] = lax.optimization_barrier((packed, far[0]))
    got[1] = gather(1, next_packed)
    next_packed, far[1] = lax.optimization_barrier((next_packed, far[1]))
    got[7] = gather(7, next_packed)
    late_device, far[2] = lax.optimization_barrier((device, far[2]))
    own_acts, far_acts = lay(
        late_device, gate_act.reshape(blocks), up_act.reshape(blocks), token_count * top
    )
    far_acts = other(far_acts)
    weights = [own[0], far[0], own[1], own[2], far[1], far[2]]
    for member, axis, first in ((6, 2, 4), (3, 1, 2), (5, 4, 1)):
        got[member] = gather(axis, got[first])
    gathered = [got[m] for m in range(MEMBERS)]

    messages = dict(zip(ORDER, pick(device, gathered, features, top, per_pair)))
    high, low = weigh(device, gathered, features, top, per_pair)

    def send(members, parts):
        return [exchange(m, part) if m else part for m, part in zip(members, parts)]

    early = send(EARLY, [messages[m] for m in EARLY])
    late, early[-1], far_acts = lax.optimization_barrier(
        ([messages[m] for m in LATE], early[-1], far_acts)
    )
    late = send(LATE, late)
    held = (own_acts, far_acts, *weights)
    early = expert(0, early, *held)
    late = expert(len(EARLY) * MEMBERS * per_pair, late, *held)
    early = send(EARLY, early)
    late = list(late)
    early[1], late[1:] = lax.optimization_barrier((early[1], late[1:]))
    late = send(LATE, late)
    sums = combine(high, low, early + late, per_pair)
    far = gather(7, sums[7]).astype(jnp.float32)
    total = sums[0]
    for member, axis, first in ((6, 2, 4), (3, 1, 2), (5, 4, 1)):
        passed = sums[first].astype(jnp.float32) + gather(axis, sums[member]).astype(jnp.float32)
        total = total + gather(first, passed.astype(jnp.bfloat16)).astype(jnp.float32)
    return (total + far).astype(jnp.bfloat16)


def solution(mesh):
    flat = Mesh(mesh.devices.reshape(-1), ("i",))
    two, three = P("i", None), P("i", None, None)
    return jax.shard_map(
        shards, mesh=flat, in_specs=(two,) * 5 + (three,) * 5, out_specs=two, check_vma=False
    )
```

```python
import functools

import jax
import jax.numpy as jnp
from jax import lax
from jax.experimental import pallas as pl
from jax.experimental.pallas import tpu as pltpu
from jax.sharding import Mesh
from jax.sharding import PartitionSpec as P

GROUP = 2
SIDE = 4
MEMBERS = 8
META = 128
LANES = 512
WIDE = 1792
AHEAD = 2
CUTS = ((0, 2048), (2048, 1536))
EARLY = (0, 3, 5, 4, 2)
LATE = (7, 6, 1)
ORDER = EARLY + LATE
VMEM = 62 * 1024 * 1024
EXPERT_VMEM = 40 * 1024 * 1024


def place_of_chip(chip):
    return (chip // 8) % SIDE, chip % SIDE, chip // 32 * 2 + chip // 4 % 2


def chip_at(x, y, z):
    return ((z // 2 * SIDE + x) * 2 + z % 2) * SIDE + y


def member_of(chip, kind, member):
    place = []
    for axis, at in enumerate(place_of_chip(chip)):
        bit = member >> (2 - axis) & 1
        place.append(((at + kind) ^ bit) - kind & SIDE - 1)
    return chip_at(*place)


def pairs(devices, swapped, member):
    found = []
    for device in range(devices):
        chip, core = divmod(device, GROUP)
        found.append((device, member_of(chip, core ^ swapped, member) * GROUP + core))
    return found


def axis_terms(device, swapped, steps):
    chip, core = device // GROUP, lax.rem(device, GROUP) ^ swapped
    places = place_of_chip(chip)
    found = []
    for axis, at in enumerate(places):
        terms = []
        for bits in range(1 << steps):
            here = ((at + (1 - core)) ^ (bits & 1)) - (1 - core) & SIDE - 1
            if steps > 1:
                here = ((here + core) ^ (bits >> 1)) - core & SIDE - 1
            terms.append(chip_at(*[here if n == axis else 0 for n in range(3)]))
        found.append(terms)
    return found


def walk(terms, member, second=0):
    return sum(
        terms[axis][(member >> (2 - axis) & 1) + 2 * (second >> (2 - axis) & 1)] for axis in range(3)
    )


def dot_nt(left, right):
    return lax.dot_general(
        left, right, (((1,), (1,)), ((), ())), preferred_element_type=jnp.float32
    )


def dot_tn(left, right):
    return lax.dot_general(
        left, right, (((0,), (0,)), ((), ())), preferred_element_type=jnp.float32
    )


def dot_nn(left, right):
    return jnp.dot(left, right, preferred_element_type=jnp.float32)


def cost(flops, moved):
    return pl.CostEstimate(flops=flops, bytes_accessed=moved, transcendentals=0)


def split(value):
    high = value.astype(jnp.bfloat16)
    return high, (value - high.astype(jnp.float32)).astype(jnp.bfloat16)


def pack_tokens(codes_ref, scales_ref, ids_ref, slots_ref, probs_ref, out_ref):
    features = codes_ref.shape[1]
    blocks = scales_ref.shape[0]
    width = features // blocks
    scales = scales_ref[...]
    for start in range(0, features, LANES):
        lane = lax.broadcasted_iota(jnp.int32, (blocks, LANES), 1) + start
        block = lax.broadcasted_iota(jnp.int32, (blocks, LANES), 0)
        spread = jnp.where(lane // width == block, 1.0, 0.0).astype(jnp.bfloat16)
        lanes = slice(start, start + LANES)
        out_ref[:, lanes] = (
            codes_ref[:, lanes].astype(jnp.float32) * dot_tn(scales, spread)
        ).astype(jnp.bfloat16)
    high, low = split(probs_ref[...])
    facts = jnp.concatenate(
        [ids_ref[...].astype(jnp.float32), slots_ref[...].astype(jnp.float32),
         high.astype(jnp.float32), low.astype(jnp.float32)], axis=0,
    ).astype(jnp.bfloat16)
    count = facts.shape[0]
    spread = jnp.where(
        lax.broadcasted_iota(jnp.int32, (count, META), 0)
        == lax.broadcasted_iota(jnp.int32, (count, META), 1), 1.0, 0.0,
    ).astype(jnp.bfloat16)
    out_ref[:, features:] = dot_tn(facts, spread).astype(jnp.bfloat16)


def pack(codes, scales, ids, slots, probs):
    tokens, features = codes.shape
    return pl.pallas_call(
        pack_tokens,
        out_shape=jax.ShapeDtypeStruct((tokens, features + META), jnp.bfloat16),
        compiler_params=pltpu.CompilerParams(vmem_limit_bytes=VMEM),
        cost_estimate=cost(2 * tokens * features * scales.shape[0], 4 * tokens * features),
    )(codes, scales, ids, slots, probs)


def lay_kernel(per_pair, device_ref, gate_act, up_act, own_out, far_out, own_ref, far_ref, in_sem, out_sem):
    rows = own_ref.shape[0] // 2
    for swapped, part, sem in ((1, far_ref, in_sem.at[1]), (0, own_ref, in_sem.at[0])):
        terms = axis_terms(device_ref[0], swapped, 2)
        core = lax.rem(device_ref[0], GROUP) ^ swapped
        for m, member in enumerate(ORDER):
            for g in range(MEMBERS):
                block = walk(terms, member, g) * GROUP + core
                at = (m * MEMBERS + g) * per_pair
                for n, act in enumerate((gate_act, up_act)):
                    pltpu.make_async_copy(
                        act.at[block], part.at[pl.ds(n * rows + at, per_pair)], sem
                    ).start()
    copies = []
    for n, (part, out) in ((1, (far_ref, far_out)), (0, (own_ref, own_out))):
        pltpu.make_async_copy(part, part, in_sem.at[n]).wait()
        copies.append(pltpu.make_async_copy(part, out, out_sem.at[n]))
        copies[-1].start()
    for copy in copies:
        copy.wait()


def lay(device, gate_act, up_act, rows):
    _, per_pair, units = gate_act.shape
    anywhere = pl.BlockSpec(memory_space=pl.ANY)
    act = jax.ShapeDtypeStruct((2 * rows, units), jnp.bfloat16)
    return pl.pallas_call(
        functools.partial(lay_kernel, per_pair),
        in_specs=[pl.BlockSpec(memory_space=pltpu.SMEM)] + [anywhere] * 2,
        out_specs=[anywhere, anywhere],
        out_shape=[act, act],
        scratch_shapes=[pltpu.VMEM(act.shape, jnp.bfloat16)] * 2
        + [pltpu.SemaphoreType.DMA((2,)), pltpu.SemaphoreType.DMA((2,))],
        compiler_params=pltpu.CompilerParams(vmem_limit_bytes=VMEM),
        cost_estimate=cost(0, 16 * rows * units),
    )(device, gate_act, up_act)


def wanted(device_ref, per_pair, rows):
    lane = lax.broadcasted_iota(jnp.int32, (1, rows), 1)
    message = lane // per_pair
    want = jnp.zeros((1, rows), jnp.int32)
    terms = axis_terms(device_ref[0], 0, 1)
    for m, member in enumerate(ORDER):
        want = jnp.where(message == m, walk(terms, member), want)
    return (want * per_pair + (lane - message * per_pair)).astype(jnp.float32)


def spread_of(meta, column, scale, top, rows):
    lane = lax.broadcasted_iota(jnp.int32, (META, top * rows), 1) // rows
    line = lax.broadcasted_iota(jnp.int32, (META, top * rows), 0)
    chosen = jnp.zeros((META, top * rows), jnp.float32)
    for first, factor in zip(column, scale):
        chosen = jnp.where(line == lane + first, factor, chosen)
    return dot_nn(meta, chosen.astype(jnp.bfloat16))


def pick_kernel(top, per_pair, device_ref, *refs):
    metas, grads = refs[:MEMBERS], refs[MEMBERS : 2 * MEMBERS]
    outs, hit_ref = refs[2 * MEMBERS : 3 * MEMBERS], refs[-1]
    rows = MEMBERS * per_pair

    @pl.when(pl.program_id(0) == 0)
    def _():
        want = wanted(device_ref, per_pair, rows)
        for g in range(MEMBERS):
            place = spread_of(metas[g][...], (0, top), (float(per_pair), 1.0), top, rows)
            hit = jnp.zeros((place.shape[0], rows), jnp.float32)
            for k in range(top):
                hit = jnp.where(place[:, k * rows : (k + 1) * rows] == want, 1.0, hit)
            hit_ref[g] = hit.T.astype(jnp.bfloat16)

    for g in range(MEMBERS):
        picked = dot_nn(hit_ref[g], grads[g][...]).astype(jnp.bfloat16)
        for m in range(MEMBERS):
            outs[m][g * per_pair : (g + 1) * per_pair, :] = picked[m * per_pair : (m + 1) * per_pair, :]


def pick(device, gathered, features, top, per_pair):
    tokens = gathered[0].shape[0]
    rows = MEMBERS * per_pair
    meta = pl.BlockSpec((tokens, META), lambda i, *_: (0, features // META))
    tile = pl.BlockSpec((tokens, WIDE), lambda i, *_: (0, i))
    out = pl.BlockSpec((rows, WIDE), lambda i, *_: (0, i))
    return pl.pallas_call(
        functools.partial(pick_kernel, top, per_pair),
        grid_spec=pltpu.PrefetchScalarGridSpec(
            num_scalar_prefetch=1,
            grid=(features // WIDE,),
            in_specs=[meta] * MEMBERS + [tile] * MEMBERS,
            out_specs=[out] * MEMBERS,
            scratch_shapes=[pltpu.VMEM((MEMBERS, rows, tokens), jnp.bfloat16)],
        ),
        out_shape=[jax.ShapeDtypeStruct((rows, features), jnp.bfloat16)] * MEMBERS,
        compiler_params=pltpu.CompilerParams(vmem_limit_bytes=VMEM),
        cost_estimate=cost(
            2 * MEMBERS * rows * tokens * features, 2 * MEMBERS * features * (rows + tokens)
        ),
    )(device, *gathered, *gathered)


def weigh_kernel(top, per_pair, device_ref, *refs):
    metas, high_ref, low_ref = refs[:MEMBERS], refs[-2], refs[-1]
    rows = MEMBERS * per_pair
    want = wanted(device_ref, per_pair, rows)
    for g in range(MEMBERS):
        meta = metas[g][...]
        place = spread_of(meta, (0, top), (float(per_pair), 1.0), top, rows)
        highs = spread_of(meta, (2 * top,), (1.0,), top, rows)
        lows = spread_of(meta, (3 * top,), (1.0,), top, rows)
        high = jnp.zeros((place.shape[0], rows), jnp.float32)
        low = jnp.zeros((place.shape[0], rows), jnp.float32)
        for k in range(top):
            lanes = slice(k * rows, (k + 1) * rows)
            hit = place[:, lanes] == want
            high = jnp.where(hit, highs[:, lanes], high)
            low = jnp.where(hit, lows[:, lanes], low)
        high_ref[g] = high.astype(jnp.bfloat16)
        low_ref[g] = low.astype(jnp.bfloat16)


def weigh(device, gathered, features, top, per_pair):
    tokens = gathered[0].shape[0]
    rows = MEMBERS * per_pair
    shape = (MEMBERS, tokens, rows)
    meta = pl.BlockSpec((tokens, META), lambda i, *_: (0, features // META))
    out = pl.BlockSpec(shape, lambda i, *_: (0, 0, 0))
    return pl.pallas_call(
        functools.partial(weigh_kernel, top, per_pair),
        grid_spec=pltpu.PrefetchScalarGridSpec(
            num_scalar_prefetch=1, grid=(1,), in_specs=[meta] * MEMBERS, out_specs=[out, out]
        ),
        out_shape=[jax.ShapeDtypeStruct(shape, jnp.bfloat16)] * 2,
        compiler_params=pltpu.CompilerParams(vmem_limit_bytes=VMEM),
        cost_estimate=cost(0, 1 << 22),
    )(device, *gathered)


def expert_kernel(first, count, *refs):
    messages, refs = refs[:count], refs[count:]
    own_acts, far_acts, down, back, refs = *refs[:2], refs[2:4], refs[4:8], refs[8:]
    outs, (rows_ref, act_ref, down_ref, back_ref, grad_ref) = refs[:count], refs[count : count + 5]
    in_sem, act_sem, down_sem, back_sem, out_sem = refs[count + 5 :]
    size = messages[0].shape[0]
    total, features = rows_ref.shape
    units = act_ref.shape[2]
    all_rows = own_acts.shape[0] // 2

    cuts = [pl.ds(*cut) for cut in CUTS]
    rows_in = [
        [
            pltpu.make_async_copy(
                ref.at[:, cut], rows_ref.at[pl.ds(m * size, size), cut], in_sem.at[c, m]
            )
            for m, ref in enumerate(messages)
        ]
        for c, cut in enumerate(cuts)
    ]
    acts_in = [
        pltpu.make_async_copy(
            ref.at[pl.ds(start + first, total)], act_ref.at[n], act_sem.at[n]
        )
        for n, (ref, start) in enumerate(
            ((own_acts, 0), (own_acts, all_rows), (far_acts, 0), (far_acts, all_rows))
        )
    ]
    down_in = [
        [
            pltpu.make_async_copy(
                ref.at[:, cut], down_ref.at[n, :, cut], down_sem.at[n, c]
            )
            for c, cut in enumerate(cuts)
        ]
        for n, ref in enumerate(down)
    ]
    back_in = [
        [
            pltpu.make_async_copy(
                ref.at[pl.ds(start, LANES)],
                back_ref.at[pl.ds(start, LANES), pl.ds(n * units, units)],
                back_sem.at[start // LANES, n],
            )
            for n, ref in enumerate(back)
        ]
        for start in range(0, features, LANES)
    ]
    for c in range(len(cuts)):
        for copy in rows_in[c] + [down_in[0][c]]:
            copy.start()
    for copy in acts_in[:2] + down_in[1] + acts_in[2:]:
        copy.start()
    for tile in back_in[:AHEAD]:
        for copy in tile:
            copy.start()

    for half in range(GROUP):
        hidden = None
        for c, cut in enumerate(cuts):
            for copy in (rows_in[c] if half == 0 else []) + [down_in[half][c]]:
                copy.wait()
            here = slice(CUTS[c][0], sum(CUTS[c]))
            term = dot_nt(rows_ref[:, here], down_ref[half, :, here])
            hidden = term if hidden is None else hidden + term
        acts_in[2 * half].wait()
        acts_in[2 * half + 1].wait()
        gate_pre = act_ref[2 * half].astype(jnp.float32)
        up_pre = act_ref[2 * half + 1].astype(jnp.float32)
        sig = 1.0 / (1.0 + jnp.exp(-gate_pre))
        here = 2 * half * units
        grad_ref[:, here : here + units] = (
            hidden * up_pre * sig * (1.0 + gate_pre * (1.0 - sig))
        ).astype(jnp.bfloat16)
        grad_ref[:, here + units : here + 2 * units] = (hidden * gate_pre * sig).astype(jnp.bfloat16)

    copies = []
    for part, tile in enumerate(back_in):
        for copy in tile:
            copy.wait()
        for later in back_in[part + AHEAD : part + AHEAD + 1]:
            for copy in later:
                copy.start()
        here = slice(part * LANES, (part + 1) * LANES)
        rows_ref[:, here] = dot_nt(grad_ref[...], back_ref[here, :]).astype(jnp.bfloat16)
        for m, ref in enumerate(outs):
            copy = pltpu.make_async_copy(
                rows_ref.at[pl.ds(m * size, size), here], ref.at[:, here], out_sem.at[part, m]
            )
            copy.start()
            copies.append(copy)
    for copy in copies:
        copy.wait()


def expert(first, messages, own_acts, far_acts, *weights):
    count = len(messages)
    size, features = messages[0].shape
    rows, units = count * size, own_acts.shape[1]
    tiles = features // LANES
    anywhere = pl.BlockSpec(memory_space=pl.ANY)
    return pl.pallas_call(
        functools.partial(expert_kernel, first, count),
        in_specs=[anywhere] * (count + 2 + len(weights)),
        out_specs=[anywhere] * count,
        out_shape=[jax.ShapeDtypeStruct((size, features), jnp.bfloat16)] * count,
        scratch_shapes=[
            pltpu.VMEM((rows, features), jnp.bfloat16),
            pltpu.VMEM((2 * GROUP, rows, units), jnp.bfloat16),
            pltpu.VMEM((GROUP, units, features), jnp.bfloat16),
            pltpu.VMEM((features, 2 * GROUP * units), jnp.bfloat16),
            pltpu.VMEM((rows, 2 * GROUP * units), jnp.bfloat16),
            pltpu.SemaphoreType.DMA((len(CUTS), count)),
            pltpu.SemaphoreType.DMA((2 * GROUP,)),
            pltpu.SemaphoreType.DMA((GROUP, len(CUTS))),
            pltpu.SemaphoreType.DMA((tiles, 2 * GROUP)),
            pltpu.SemaphoreType.DMA((tiles, count)),
        ],
        compiler_params=pltpu.CompilerParams(vmem_limit_bytes=EXPERT_VMEM),
        cost_estimate=cost(
            12 * rows * features * units,
            4 * rows * features + 8 * rows * units + 12 * units * features,
        ),
    )(*messages, own_acts, far_acts, *weights)


def combine_kernel(per_pair, high_ref, low_ref, *refs):
    messages, outs = refs[:MEMBERS], refs[MEMBERS:]
    for g in range(MEMBERS):
        rows = jnp.concatenate(
            [message[g * per_pair : (g + 1) * per_pair, :] for message in messages], axis=0
        )
        total = dot_nn(high_ref[g], rows) + dot_nn(low_ref[g], rows)
        outs[g][...] = total.astype(outs[g].dtype)


def combine(high, low, messages, per_pair):
    rows, features = messages[0].shape
    tokens = high.shape[1]
    whole = pl.BlockSpec(high.shape, lambda i: (0, 0, 0))
    tile = pl.BlockSpec((rows, WIDE), lambda i: (0, i))
    out = pl.BlockSpec((tokens, WIDE), lambda i: (0, i))
    return pl.pallas_call(
        functools.partial(combine_kernel, per_pair),
        grid=(features // WIDE,),
        in_specs=[whole, whole] + [tile] * MEMBERS,
        out_specs=[out] * MEMBERS,
        out_shape=[
            jax.ShapeDtypeStruct((tokens, features), jnp.float32 if g == 0 else jnp.bfloat16)
            for g in range(MEMBERS)
        ],
        compiler_params=pltpu.CompilerParams(vmem_limit_bytes=36 * 1024 * 1024),
        cost_estimate=cost(
            4 * MEMBERS * rows * tokens * features, 2 * MEMBERS * features * (rows + tokens)
        ),
    )(high, low, *messages)


def shards(
    grad_codes, grad_scales, expert_ids, slots, gate_probs,
    gate_act, up_act, gate_weight, up_weight, down_weight,
):
    token_count, features = grad_codes.shape
    top = expert_ids.shape[1]
    devices = lax.axis_size("i")
    per_pair = token_count * top // (devices // GROUP)
    hidden = gate_act.shape[2]
    device = lax.axis_index("i").reshape(1)

    def within(swapped, member, value):
        return lax.ppermute(value, "i", pairs(devices, swapped, member))

    gather = functools.partial(within, 0)
    exchange = functools.partial(within, 1)

    def other(value):
        return lax.ppermute(value, "i", [(d, d ^ 1) for d in range(devices)])

    blocks = (devices, per_pair, hidden)
    packed = pack(grad_codes, grad_scales.T, expert_ids.T, slots.T, gate_probs.T)
    own = [down_weight[0], gate_weight[0], up_weight[0]]
    far = [other(w) for w in own]
    got = {0: packed, 4: gather(4, packed), 2: gather(2, packed)}
    next_packed, far[0] = lax.optimization_barrier((packed, far[0]))
    got[1] = gather(1, next_packed)
    next_packed, far[1] = lax.optimization_barrier((next_packed, far[1]))
    got[7] = gather(7, next_packed)
    late_device, far[2] = lax.optimization_barrier((device, far[2]))
    own_acts, far_acts = lay(
        late_device, gate_act.reshape(blocks), up_act.reshape(blocks), token_count * top
    )
    far_acts = other(far_acts)
    weights = [own[0], far[0], own[1], own[2], far[1], far[2]]
    for member, axis, first in ((6, 2, 4), (3, 1, 2), (5, 4, 1)):
        got[member] = gather(axis, got[first])
    gathered = [got[m] for m in range(MEMBERS)]

    messages = dict(zip(ORDER, pick(device, gathered, features, top, per_pair)))
    high, low = weigh(device, gathered, features, top, per_pair)

    def send(members, parts):
        return [exchange(m, part) if m else part for m, part in zip(members, parts)]

    early = send(EARLY, [messages[m] for m in EARLY])
    late, early[-1], far_acts = lax.optimization_barrier(
        ([messages[m] for m in LATE], early[-1], far_acts)
    )
    late = send(LATE, late)
    held = (own_acts, far_acts, *weights)
    early = expert(0, early, *held)
    late = expert(len(EARLY) * MEMBERS * per_pair, late, *held)
    early = send(EARLY, early)
    late = send(LATE, late)
    sums = combine(high, low, early + late, per_pair)
    far = gather(7, sums[7]).astype(jnp.float32)
    total = sums[0]
    for member, axis, first in ((6, 2, 4), (3, 1, 2), (5, 4, 1)):
        passed = sums[first].astype(jnp.float32) + gather(axis, sums[member]).astype(jnp.float32)
        total = total + gather(first, passed.astype(jnp.bfloat16)).astype(jnp.float32)
    return (total + far).astype(jnp.bfloat16)


def solution(mesh):
    flat = Mesh(mesh.devices.reshape(-1), ("i",))
    two, three = P("i", None), P("i", None, None)
    return jax.shard_map(
        shards, mesh=flat, in_specs=(two,) * 5 + (three,) * 5, out_specs=two, check_vma=False
    )
```
